512 devices in a mesh: dp: 8 (over y_hi, core), fsdp: 64 (over x, z, y_lo).
Axes of the slice: x: 4, y: 8 (y_hi: 4, y_lo: 2; y = y_hi * 2 + y_lo), z: 8, core: 2. Of those that a mesh axis runs over, the one named last changes fastest.
Arguments:
- tokens: bfloat16 [65536, 4096], P(('dp', 'fsdp')), may hold values from -6 to 6
- out_grad: bfloat16 [65536, 14336], P(('dp', 'fsdp')), may hold values from -0.01171875 to 0.01171875
- basis: bfloat16 [4096, 64], P('fsdp'), may hold values from -0.75 to 0.75
- first_moment: float32 [64, 14336], P('dp', 'fsdp'), may hold values from -0.6 to 0.6
- second_moment: float32 [64, 14336], P('dp', 'fsdp'), may hold values from 0.0005 to 0.002
Outputs:
- update: bfloat16 [4096, 14336], P('fsdp', 'dp')
- new_first: float32 [64, 14336], P('dp', 'fsdp')
- new_second: float32 [64, 14336], P('dp', 'fsdp')
The draws below stay inside these ranges and needn't reach their ends.
All inputs are finite; a program needn't handle non-finite values.
Results may differ from the reference program's by a relative error of at most 0.0048.
Values may be sent and summed in bfloat16 or wider, within the bound.
A program may use at most 64 MiB of HBM per device.

```python
import math
import jax
import jax.numpy as jnp
from jax import lax

D = 4096
F = 14336
R = 64
TOKENS = 65536


def with_spikes(entries, stream_key, source, target, blocks, factor):
    owner, partner = [(jnp.arange(entries.shape[position]) // (entries.shape[position] // blocks)).reshape([-1 if axis == position else 1 for axis in range(entries.ndim)]) for position in (source, target)]
    chosen = jax.random.permutation(stream_key, blocks)[partner]
    strong = (owner == chosen) | (owner == (partner + blocks // 2) % blocks)
    return jnp.where(strong, factor * entries, entries)


def steps_of(rng, shape, split, smallest, largest):
    def one(dim, parts):
        steps = jax.random.uniform(jax.random.fold_in(jax.random.fold_in(rng, 6), dim), (parts,), jnp.float32, smallest / len(split), largest / len(split))
        return jnp.repeat(jnp.exp(steps), shape[dim] // parts).reshape((-1,) + (1,) * (len(shape) - dim - 1))

    loudness = one(*split[0])
    for cut in split[1:]:
        loudness = loudness * one(*cut)
    return loudness


def gaussian(own_key, shape, width, reach, pieces=(), kind=jnp.bfloat16):
    entries = jax.random.normal(own_key, shape, jnp.float32) * width
    if len(pieces) > 0:
        entries = steps_of(own_key, shape, pieces, -0.22, 0.18) * entries
    return jnp.clip(entries, min=-reach, max=reach).astype(kind)


def gaussian_with(stream_key, shape, width, limit, pieces, heavy, dtype=jnp.bfloat16):
    drawn = width * jax.random.normal(stream_key, shape, jnp.float32)
    if pieces:
        drawn = drawn * steps_of(stream_key, shape, pieces, -0.22, 0.18)
    return jnp.clip(with_spikes(drawn, jax.random.fold_in(stream_key, 3), *heavy), -limit, limit).astype(dtype)


def setup_inputs(seed: int = 0) -> dict:
    seeds = jax.random.split(jax.random.key(seed), 6)
    return {
        "tokens": gaussian(seeds[0], (TOKENS, D), 1.0, 6.0, ((0, 512),)),
        "out_grad": gaussian_with(seeds[1], (TOKENS, F), ((TOKENS * (D // R)) ** -0.5), 0.01171875, ((0, 512),), (0, 1, 512, 6.0)),
        "basis": gaussian(seeds[2], (D, R), R ** -0.5, 0.75, ((0, 64),)),
        "first_moment": gaussian(seeds[3], (R, F), 0.1, 0.6, ((0, 8), (1, 64)), jnp.float32),
        "second_moment": jnp.clip(jnp.exp(math.log(0.002) - 1.3862944 * jax.random.uniform(seeds[4], (R, F), jnp.float32) ** steps_of(seeds[4], (R, F), ((0, 8), (1, 64)), -0.2, 0.2)), 0.0005, 0.002),
    }


beta_one = 0.9
beta_two = 0.999
corr_one = 1.0 - 0.9 ** 10
corr_two = 1.0 - 0.999 ** 10
adam_eps = 1e-08
step_rate = 4.0

def reference(tokens, out_grad, basis, first_moment, second_moment):
    coords = jnp.dot(tokens, basis, preferred_element_type=jnp.float32).astype(jnp.bfloat16)
    grad = lax.dot_general(coords, out_grad, (((0,), (0,)), ((), ())), preferred_element_type=jnp.float32)
    new_first = beta_one * first_moment + (1.0 - beta_one) * grad
    new_second = beta_two * second_moment + (1.0 - beta_two) * grad * grad
    step = new_first / corr_one / (jnp.sqrt(new_second / corr_two) + adam_eps)
    update = -step_rate * jnp.dot(basis.astype(jnp.float32), step, precision=lax.Precision.HIGHEST)
    return (update.astype(jnp.bfloat16), new_first, new_second)
```

```python
import jax
import jax.numpy as jnp
from jax import lax
from jax.experimental import pallas as pl
from jax.experimental.pallas import tpu as pltpu
from jax.sharding import PartitionSpec as P

beta_one = 0.9
beta_two = 0.999
corr_one = 1.0 - 0.9**10
corr_two = 1.0 - 0.999**10
adam_eps = 1e-08
step_rate = 4.0

F32, BF16 = jnp.float32, jnp.bfloat16
NX, NY, NZ = 4, 8, 8
TOK = 128
D = 4096
RANK = 64
SPAN = 1792
UNIT = 224
WIN = 512
STARTS = (0, 3, 7, 10)


def kernel(
    tok_in, og_in, basis_in, first_in, second_in,
    upd_out, first_out, second_out,
    tok, og, bag, cot, g, xr, zs, zr, ys, yr, sag, mom, new,
    ld_sem, core_send, core_recv, og_recv, ag_send, ag_recv, cot_send, cot_recv,
    x_send, x_recv, z_send, z_recv, y_send, y_recv, mom_send, mom_recv, new_send, new_recv,
):
    d = lax.axis_index("dp")
    f = lax.axis_index("fsdp")
    h, c = d // 2, d % 2
    x, z, p = f // 16, (f // 2) % 8, f % 2
    y = 2 * h + p
    oc = 1 - c

    def dev(x_, y_, z_, c_):
        return ((y_ // 2) * 2 + c_, (x_ * 8 + z_) * 2 + y_ % 2)

    swap = dev(h, 2 * x + p, 4 * c + z % 4, z // 4)
    alone = jnp.logical_and(x == h, z // 4 == c)
    apart = jnp.logical_not(alone)
    other = dev(x, y, z, oc)
    zp = [dev(x, 2 * h + (p + o % 2) % 2, (z + o // 2) % 8, c) for o in range(16)]
    xs = [dev((x + o) % 4, y, z, c) for o in range(4)]

    def remote(src, dst, send, recv, target):
        return pltpu.make_async_remote_copy(
            src_ref=src, dst_ref=dst, send_sem=send, recv_sem=recv,
            device_id=target, device_id_type=pl.DeviceIdType.MESH,
        )

    def await_bytes(ref, sem):
        pltpu.make_async_copy(ref, ref, sem).wait()

    mine = pl.ds(pl.multiple_of(c * TOK, TOK), TOK)
    pltpu.make_async_copy(tok_in, tok.at[mine], ld_sem.at[0]).start()
    for q in range(4):
        cols = pl.ds(pl.multiple_of((2 * q + c) * SPAN, 128), SPAN)
        pltpu.make_async_copy(og_in.at[:, cols], og.at[q, mine], ld_sem.at[1]).start()

    barrier = pltpu.get_barrier_semaphore()

    def greet(target):
        pl.semaphore_signal(barrier, inc=1, device_id=target, device_id_type=pl.DeviceIdType.MESH)

    for o in range(1, 16):
        greet(zp[o])
    for o in range(1, 4):
        greet(xs[o])
    for a in range(1, 4):
        for r in range(2):
            greet(dev(x, 2 * ((h + a) % 4) + r, z, c))
    greet(other)

    @pl.when(apart)
    def _():
        greet(swap)

    bt = jnp.transpose(basis_in[...].astype(F32))
    pieces = [bt[16 * i : 16 * i + 16] for i in range(4)]
    low = jnp.where(c == 0, pieces[0], pieces[2])
    high = jnp.where(c == 0, pieces[1], pieces[3])
    bag[x, 2 * z + p] = jnp.concatenate([low, high], axis=1).astype(BF16)

    pl.semaphore_wait(barrier, jnp.where(alone, 25, 26))

    def gather_start(buf, k):
        slot = buf.at[x, 2 * z + p]
        for o in range(1, 16):
            remote(slot, slot, ag_send.at[k, 0], ag_recv.at[k, 0], zp[o]).start()

    def gather_finish(buf, k):
        await_bytes(buf.at[0, pl.ds(0, 15)], ag_recv.at[k, 0])
        for o in range(1, 4):
            remote(buf.at[x], buf.at[x], ag_send.at[k, 1], ag_recv.at[k, 1], xs[o]).start()
        await_bytes(buf.at[pl.ds(0, 3)], ag_recv.at[k, 1])

    gather_start(bag, 0)
    remote(tok_in, tok.at[mine], core_send.at[0], core_recv.at[0], other).start()
    for q in range(4):
        cols = pl.ds(pl.multiple_of((2 * q + oc) * SPAN, 128), SPAN)
        remote(og_in.at[:, cols], og.at[q, mine], core_send.at[1], og_recv.at[q], other).start()

    @pl.when(apart)
    def _():
        remote(first_in, mom.at[0], mom_send.at[0], mom_recv.at[0], swap).start()
        remote(second_in, mom.at[1], mom_send.at[1], mom_recv.at[1], swap).start()

    @pl.when(alone)
    def _():
        mom[0] = first_in[...]
        mom[1] = second_in[...]

    gather_finish(bag, 0)
    await_bytes(tok.at[mine], ld_sem.at[0])
    await_bytes(tok.at[mine], core_recv.at[0])

    lane = lax.broadcasted_iota(jnp.int32, (16, 128), 1)
    tops, bottoms = [], []
    for k in range(32):
        even = bag[k // 8, 2 * (k % 8)].astype(F32)
        odd = bag[k // 8, 2 * (k % 8) + 1].astype(F32)
        tops.append(jnp.where(lane < 64, even, pltpu.roll(odd, 64, axis=1)).astype(BF16))
        bottoms.append(jnp.where(lane < 64, pltpu.roll(even, 64, axis=1), odd).astype(BF16))
    basis_t = jnp.concatenate(
        [jnp.concatenate(tops, axis=1), jnp.concatenate(bottoms, axis=1)], axis=0
    )
    half = lax.dot_general(
        basis_t, tok[...], (((1,), (1,)), ((), ())), preferred_element_type=F32
    )
    cot[c] = half.astype(BF16)
    remote(cot.at[c], cot.at[c], cot_send, cot_recv, other).start()
    await_bytes(cot.at[c], cot_recv)
    coords_t = cot[...].reshape(RANK, 2 * TOK)

    await_bytes(og.at[:, mine], ld_sem.at[1])
    for q in range(4):
        await_bytes(og.at[q, mine], og_recv.at[q])
        part = jnp.dot(coords_t, og[q], preferred_element_type=F32).astype(BF16)
        for i in range(4):
            g[q, i] = part[16 * i : 16 * i + 16]
        for o in (2, 1, 3):
            remote(
                g.at[q, (x + o) % 4], xr.at[q, o - 1], x_send.at[q], x_recv.at[q], xs[o]
            ).start()

    for pair in range(2):
        sums = []
        for q in (2 * pair, 2 * pair + 1):
            await_bytes(xr.at[q], x_recv.at[q])
            total = g[q, x].astype(F32)
            for o in range(3):
                total = total + xr[q, o].astype(F32)
            sums.append(total)
        for to in range(8):
            s, start = to // 4, 128 * STARTS[to % 4]
            zs[pair, to] = jnp.concatenate(
                [t[8 * s : 8 * s + 8, start : start + WIN] for t in sums], axis=0
            ).astype(BF16)
        for o in (4, 3, 5, 2, 6, 1, 7):
            to = (z + o) % 8
            remote(
                zs.at[pair, to], zr.at[pair, o - 1], z_send.at[pair], z_recv.at[pair],
                dev(x, y, to, c),
            ).start()

    for pair in range(2):
        await_bytes(zr.at[pair], z_recv.at[pair])
        total = zs[pair, z].astype(F32)
        for o in range(7):
            total = total + zr[pair, o].astype(F32)
        for j in range(2):
            for r in range(2):
                to = 2 * (2 * pair + j) + r
                ys[to] = total[8 * j : 8 * j + 8, 128 * r : 128 * r + 384]
    for o in (4, 3, 5, 2, 6, 1, 7):
        to = (y + o) % 8
        remote(ys.at[to], yr.at[o - 1], y_send, y_recv, dev(x, to, z, c)).start()

    row = lax.broadcasted_iota(jnp.int32, (RANK, 128), 0)
    col = lax.broadcasted_iota(jnp.int32, (RANK, 128), 1)
    spread = []
    for s in range(2):
        hit = col == (row // 8) * 16 + row % 8 + 8 * s
        spread.append(jnp.where(hit, -step_rate, 0.0).astype(BF16))
    left = jnp.concatenate(
        [
            jnp.dot(basis_in[...], e, preferred_element_type=F32).astype(BF16)
            for e in spread
        ],
        axis=0,
    )

    @pl.when(apart)
    def _():
        await_bytes(mom.at[0], mom_recv.at[0])
        await_bytes(mom.at[1], mom_recv.at[1])

    await_bytes(yr, y_recv)
    total = ys[y]
    for o in range(7):
        total = total + yr[o]
    shift = (z % 2) * 64 + p * 96
    grad = pltpu.roll(total, 384 - shift, axis=1)[:, :UNIT]
    new_first = beta_one * mom[0] + (1.0 - beta_one) * grad
    new_second = beta_two * mom[1] + (1.0 - beta_two) * grad * grad
    step = new_first / corr_one / (jnp.sqrt(new_second / corr_two) + adam_eps)
    step = jnp.concatenate([step, jnp.zeros((8, 256 - UNIT), F32)], axis=1)
    step = pltpu.roll(step, (96 * (2 * z + p)) % 128, axis=1)
    sag[x, 2 * z + p] = jnp.concatenate([step[:, :128], step[:, 128:]], axis=0).astype(BF16)
    gather_start(sag, 1)
    new[0] = new_first
    new[1] = new_second

    @pl.when(apart)
    def _():
        remote(new.at[0], first_out, new_send.at[0], new_recv.at[0], swap).start()
        remote(new.at[1], second_out, new_send.at[1], new_recv.at[1], swap).start()

    @pl.when(alone)
    def _():
        first_out[...] = new[0]
        second_out[...] = new[1]

    gather_finish(sag, 1)

    lane = lax.broadcasted_iota(jnp.int32, (RANK, 128), 1)
    right = jnp.concatenate(
        [
            jnp.concatenate([sag[i // 2, 8 * (i % 2) + j] for i in range(8)], axis=0)
            for j in range(8)
        ],
        axis=1,
    )
    both = jnp.dot(left, right, preferred_element_type=F32)
    low = [both[:RANK, 128 * j : 128 * j + 128] for j in range(8)]
    high = [both[RANK:, 128 * j : 128 * j + 128] for j in range(8)]
    for b in range(2):
        l, u = low[4 * b : 4 * b + 4], high[4 * b : 4 * b + 4]
        tiles = [
            l[0],
            jnp.where(lane < 96, u[0], l[1]),
            u[1],
            jnp.where(lane < 64, l[1], l[2]),
            u[2],
            jnp.where(lane < 32, l[2], l[3]),
            u[3],
        ]
        for t, tile in enumerate(tiles):
            upd_out[:, 128 * (7 * b + t) : 128 * (7 * b + t) + 128] = tile.astype(BF16)

    for k, buf in ((0, bag), (1, sag)):
        await_bytes(buf.at[0, pl.ds(0, 15)], ag_send.at[k, 0])
        await_bytes(buf.at[pl.ds(0, 3)], ag_send.at[k, 1])
    await_bytes(tok.at[mine], core_send.at[0])
    await_bytes(og.at[:, mine], core_send.at[1])
    await_bytes(cot.at[c], cot_send)
    for q in range(4):
        await_bytes(xr.at[q], x_send.at[q])
    for pair in range(2):
        await_bytes(zr.at[pair], z_send.at[pair])
    await_bytes(yr, y_send)

    @pl.when(apart)
    def _():
        for i, out in enumerate((first_out, second_out)):
            await_bytes(mom.at[i], mom_send.at[i])
            await_bytes(new.at[i], new_send.at[i])
            await_bytes(out, new_recv.at[i])


def per_device(tokens, out_grad, basis, first_moment, second_moment):
    vmem = pl.BlockSpec(memory_space=pltpu.VMEM)
    anywhere = pl.BlockSpec(memory_space=pl.ANY)
    dma = pltpu.SemaphoreType.DMA
    return pl.pallas_call(
        kernel,
        out_shape=(
            jax.ShapeDtypeStruct((RANK, SPAN), BF16),
            jax.ShapeDtypeStruct((8, UNIT), F32),
            jax.ShapeDtypeStruct((8, UNIT), F32),
        ),
        in_specs=[anywhere, anywhere, vmem, vmem, vmem],
        out_specs=[vmem, vmem, vmem],
        scratch_shapes=[
            pltpu.VMEM((2 * TOK, D), BF16),
            pltpu.VMEM((4, 2 * TOK, SPAN), BF16),
            pltpu.VMEM((NX, 16, 16, 128), BF16),
            pltpu.VMEM((2, RANK // 2, 2 * TOK), BF16),
            pltpu.VMEM((4, NX, 16, SPAN), BF16),
            pltpu.VMEM((4, NX - 1, 16, SPAN), BF16),
            pltpu.VMEM((2, NZ, 16, WIN), BF16),
            pltpu.VMEM((2, NZ - 1, 16, WIN), BF16),
            pltpu.VMEM((NY, 8, 384), F32),
            pltpu.VMEM((NY - 1, 8, 384), F32),
            pltpu.VMEM((NX, 16, 16, 128), BF16),
            pltpu.VMEM((2, 8, UNIT), F32),
            pltpu.VMEM((2, 8, UNIT), F32),
            dma((2,)),
            dma((2,)), dma((1,)), dma((4,)),
            dma((2, 2)), dma((2, 2)),
            dma, dma,
            dma((4,)), dma((4,)),
            dma((2,)), dma((2,)),
            dma, dma,
            dma((2,)), dma((2,)),
            dma((2,)), dma((2,)),
        ],
        compiler_params=pltpu.CompilerParams(
            collective_id=0, has_side_effects=True, vmem_limit_bytes=48 << 20
        ),
    )(tokens, out_grad, basis, first_moment, second_moment)


def solution(mesh):
    placed = (
        P(("dp", "fsdp"), None),
        P(("dp", "fsdp"), None),
        P("fsdp", None),
        P("dp", "fsdp"),
        P("dp", "fsdp"),
    )
    return jax.shard_map(
        per_device,
        mesh=mesh,
        in_specs=placed,
        out_specs=(P("fsdp", "dp"), P("dp", "fsdp"), P("dp", "fsdp")),
        check_vma=False,
    )
```

```python
import jax
import jax.numpy as jnp
from jax import lax
from jax.experimental import pallas as pl
from jax.experimental.pallas import tpu as pltpu
from jax.sharding import PartitionSpec as P

beta_one = 0.9
beta_two = 0.999
corr_one = 1.0 - 0.9**10
corr_two = 1.0 - 0.999**10
adam_eps = 1e-08
step_rate = 4.0

F32, BF16 = jnp.float32, jnp.bfloat16
NX, NY, NZ = 4, 8, 8
TOK = 128
D = 4096
RANK = 64
SPAN = 1792
UNIT = 224
WIN = 512
STARTS = (0, 3, 7, 10)
FAR = (4, 3, 5, 2, 6, 1, 7)


def await_bytes(ref, sem):
    pltpu.make_async_copy(ref, ref, sem).wait()


def kernel(
    tok_in, og_in, basis_in, first_in, second_in,
    sag, new_out,
    bas, tok, og, bag, cot, g, xr, zs, zr, zs2, zr2, zs3, zr3, xs3, xr3, ys, yr, tile, mom, new,
    ld_sem, core_send, core_recv, og_recv, ag_send, ag_recv, fw_send, fw_recv, cot_send, cot_recv,
    x_send, x_recv, z_send, z_recv, y_send, y_recv, mom_send, mom_recv, new_send, new_recv,
    st_send, st_recv, st_own, ready,
):
    d = lax.axis_index("dp")
    f = lax.axis_index("fsdp")
    h, c = d // 2, d % 2
    x, z, p = f // 16, (f // 2) % 8, f % 2
    y = 2 * h + p
    oc = 1 - c

    def dev(x_, y_, z_, c_):
        return ((y_ // 2) * 2 + c_, (x_ * 8 + z_) * 2 + y_ % 2)

    swap = dev(h, 2 * x + p, 4 * c + z % 4, z // 4)
    alone = jnp.logical_and(x == h, z // 4 == c)
    apart = jnp.logical_not(alone)
    other = dev(x, y, z, oc)
    xs = [dev((x + o) % 4, y, z, c) for o in range(4)]

    def plane(a, b, s):
        return dev((x + a) % 4, 2 * h + (p + s) % 2, (z + b) % 8, c)

    def remote(src, dst, send, recv, target):
        return pltpu.make_async_remote_copy(
            src_ref=src, dst_ref=dst, send_sem=send, recv_sem=recv,
            device_id=target, device_id_type=pl.DeviceIdType.MESH,
        )

    def signal(sem, target):
        pl.semaphore_signal(sem, inc=1, device_id=target, device_id_type=pl.DeviceIdType.MESH)

    barrier = pltpu.get_barrier_semaphore()
    pltpu.make_async_copy(basis_in, bas, ld_sem.at[2]).start()
    for b in FAR + (0,):
        for s in (1, 0):
            if (b, s) != (0, 0):
                signal(barrier, plane(0, b, s))
    for a in (2, 1, 3):
        for r in range(2):
            signal(barrier, dev(x, 2 * ((h + a) % 4) + r, z, c))
    for o in (2, 1, 3):
        signal(barrier, xs[o])
    signal(barrier, other)

    mine = pl.ds(pl.multiple_of(c * TOK, TOK), TOK)
    pltpu.make_async_copy(tok_in, tok.at[mine], ld_sem.at[0]).start()
    for q in range(4):
        cols = pl.ds(pl.multiple_of((2 * q + c) * SPAN, 128), SPAN)
        pltpu.make_async_copy(og_in.at[:, cols], og.at[q, mine], ld_sem.at[1]).start()

    await_bytes(bas, ld_sem.at[2])
    bt = jnp.transpose(bas[...].astype(F32))
    pieces = [bt[16 * i : 16 * i + 16] for i in range(4)]
    low = jnp.where(c == 0, pieces[0], pieces[2])
    high = jnp.where(c == 0, pieces[1], pieces[3])
    bag[f] = jnp.concatenate([low, high], axis=1).astype(BF16)

    pl.semaphore_wait(barrier, 25)

    for b in FAR + (0,):
        for s in (1, 0):
            if (b, s) != (0, 0):
                remote(bag.at[f], bag.at[f], ag_send, ag_recv.at[b], plane(0, b, s)).start()
    remote(tok_in, tok.at[mine], core_send.at[0], core_recv, other).start()
    for q in (0, 3, 1, 2):
        cols = pl.ds(pl.multiple_of((2 * q + oc) * SPAN, 128), SPAN)
        remote(og_in.at[:, cols], og.at[q, mine], core_send.at[1], og_recv.at[q], other).start()
    for b in (0, 1, 7, 2, 6, 3, 5, 4):
        await_bytes(bag.at[pl.ds(0, 2 if b else 1)], ag_recv.at[b])
        pair = bag.at[pl.ds(16 * x + 2 * ((z + 8 - b) % 8), 2)]
        for o in (2, 1, 3):
            remote(pair, pair, fw_send, fw_recv.at[o - 1], xs[o]).start()

    await_bytes(tok.at[mine], ld_sem.at[0])
    await_bytes(tok.at[mine], core_recv)
    lane = lax.broadcasted_iota(jnp.int32, (16, 128), 1)
    half = None
    for o in (0, 1, 3, 2):
        at = (x + 4 - o) % 4
        if o:
            await_bytes(bag.at[pl.ds(0, 16)], fw_recv.at[o - 1])
        tops, bottoms = [], []
        for k in range(8):
            even = bag[16 * at + 2 * k].astype(F32)
            odd = bag[16 * at + 2 * k + 1].astype(F32)
            tops.append(jnp.where(lane < 64, even, pltpu.roll(odd, 64, axis=1)).astype(BF16))
            bottoms.append(jnp.where(lane < 64, pltpu.roll(even, 64, axis=1), odd).astype(BF16))
        basis_t = jnp.concatenate(
            [jnp.concatenate(tops, axis=1), jnp.concatenate(bottoms, axis=1)], axis=0
        )
        term = lax.dot_general(
            basis_t,
            tok[:, pl.ds(pl.multiple_of(1024 * at, 1024), 1024)],
            (((1,), (1,)), ((), ())),
            preferred_element_type=F32,
        )
        half = term if half is None else half + term
    cot[c] = half.astype(BF16)
    remote(cot.at[c], cot.at[c], cot_send, cot_recv, other).start()
    await_bytes(cot.at[c], cot_recv)
    coords_t = cot[...].reshape(RANK, 2 * TOK)

    await_bytes(og.at[:, mine], ld_sem.at[1])
    for q in (0, 3, 1, 2):
        await_bytes(og.at[q, mine], og_recv.at[q])
        part = jnp.dot(coords_t, og[q], preferred_element_type=F32)
        if q == 3:
            for to in range(8):
                s, start = to // 4, 128 * STARTS[to % 4]
                zs3[to] = jnp.concatenate(
                    [part[16 * i + 8 * s : 16 * i + 8 * s + 8, start : start + WIN] for i in range(4)],
                    axis=0,
                ).astype(BF16)
            for o in FAR:
                to = (z + o) % 8
                remote(
                    zs3.at[to], zr3.at[o - 1], z_send.at[2], z_recv.at[2], dev(x, y, to, c)
                ).start()
        else:
            part = part.astype(BF16)
            for i in range(4):
                g[q, i] = part[16 * i : 16 * i + 16]
            for o in (2, 1, 3):
                remote(
                    g.at[q, (x + o) % 4], xr.at[q, o - 1], x_send.at[q], x_recv.at[q], xs[o]
                ).start()

    for o in FAR:
        signal(ready, dev(x, (y + o) % 8, z, c))

    def along_x(q):
        await_bytes(xr.at[q], x_recv.at[q])
        total = g[q, x].astype(F32)
        for o in range(3):
            total = total + xr[q, o].astype(F32)
        return total

    sums = [along_x(0), along_x(1)]
    for to in range(8):
        s, start = to // 4, 128 * STARTS[to % 4]
        zs[to] = jnp.concatenate(
            [t[8 * s : 8 * s + 8, start : start + WIN] for t in sums], axis=0
        ).astype(BF16)
    for o in FAR:
        to = (z + o) % 8
        remote(zs.at[to], zr.at[o - 1], z_send.at[0], z_recv.at[0], dev(x, y, to, c)).start()

    await_bytes(zr3, z_recv.at[2])
    total = zs3[z].astype(F32)
    for o in range(7):
        total = total + zr3[o].astype(F32)
    for i in range(4):
        xs3[i] = total[8 * i : 8 * i + 8]
    for o in (2, 1, 3):
        remote(xs3.at[(x + o) % 4], xr3.at[o - 1], x_send.at[3], x_recv.at[3], xs[o]).start()

    total = along_x(2)
    for to in range(8):
        s, start = to // 4, 128 * STARTS[to % 4]
        rows = total[8 * s : 8 * s + 8]
        zs2[to] = jnp.concatenate(
            [rows[:, start : start + 256], rows[:, start + 256 : start + 512]], axis=0
        ).astype(BF16)
    for o in FAR:
        to = (z + o) % 8
        remote(zs2.at[to], zr2.at[o - 1], z_send.at[1], z_recv.at[1], dev(x, y, to, c)).start()

    pl.semaphore_wait(ready, 7)

    @pl.when(apart)
    def _():
        remote(first_in, mom.at[0], mom_send.at[0], mom_recv.at[0], swap).start()
        remote(second_in, mom.at[1], mom_send.at[1], mom_recv.at[1], swap).start()

    @pl.when(alone)
    def _():
        pltpu.make_async_copy(first_in, mom.at[0], mom_recv.at[0]).start()
        pltpu.make_async_copy(second_in, mom.at[1], mom_recv.at[1]).start()

    def along_y(total, q):
        total = pltpu.roll(total, 512 - 64 * (z % 2), axis=1)
        blocks = [total[:, :256], pltpu.roll(total, 512 - UNIT, axis=1)[:, :256]]
        for r in range(2):
            to = 2 * q + r
            ys[to] = blocks[r]

            @pl.when(y != to)
            def _():
                slot = (to + 8 - y) % 8 - 1
                remote(ys.at[to], yr.at[slot], y_send, y_recv, dev(x, to, z, c)).start()

    await_bytes(xr3, x_recv.at[3])
    total = xs3[x]
    for o in range(3):
        total = total + xr3[o]
    along_y(total, 3)

    await_bytes(zr, z_recv.at[0])
    total = zs[z].astype(F32)
    for o in range(7):
        total = total + zr[o].astype(F32)
    along_y(total[:8], 0)
    along_y(total[8:], 1)

    await_bytes(zr2, z_recv.at[1])
    total = zs2[z].astype(F32)
    for o in range(7):
        total = total + zr2[o].astype(F32)
    along_y(jnp.concatenate([total[:8], total[8:]], axis=1), 2)

    await_bytes(mom.at[0], mom_recv.at[0])
    await_bytes(mom.at[1], mom_recv.at[1])
    await_bytes(yr, y_recv)
    total = ys[y]
    for o in range(7):
        total = total + yr[o]
    grad = total[:, :UNIT]
    new_first = beta_one * mom[0] + (1.0 - beta_one) * grad
    new_second = beta_two * mom[1] + (1.0 - beta_two) * grad * grad
    new[0] = new_first
    new[1] = new_second

    @pl.when(apart)
    def _():
        remote(new, new_out, new_send, new_recv, swap).start()

    @pl.when(alone)
    def _():
        pltpu.make_async_copy(new, new_out, new_recv).start()

    step = new_first / corr_one / (jnp.sqrt(new_second / corr_two) + adam_eps)
    step = jnp.concatenate([step, jnp.zeros((8, 256 - UNIT), F32)], axis=1)
    step = pltpu.roll(step, (96 * (2 * z + p)) % 128, axis=1)
    tile[...] = jnp.concatenate([step[:, :128], step[:, 128:]], axis=0).astype(BF16)
    offsets = [(a, b, s) for a in range(4) for b in range(8) for s in range(2)][1:]
    offsets.sort(key=lambda o: -(min(o[0], 4 - o[0]) + min(o[1], 8 - o[1]) + o[2]))
    for o in offsets:
        remote(tile, sag.at[f], st_send, st_recv, plane(*o)).start()
    pltpu.make_async_copy(tile, sag.at[f], st_own).start()

    await_bytes(bag.at[pl.ds(0, 15)], ag_send)
    await_bytes(bag.at[pl.ds(0, 48)], fw_send)
    await_bytes(tok.at[mine], core_send.at[0])
    await_bytes(og.at[:, mine], core_send.at[1])
    await_bytes(cot.at[c], cot_send)
    for q in range(3):
        await_bytes(xr.at[q], x_send.at[q])
    await_bytes(xr3, x_send.at[3])
    await_bytes(zr, z_send.at[0])
    await_bytes(zr2, z_send.at[1])
    await_bytes(zr3, z_send.at[2])
    await_bytes(yr, y_send)

    @pl.when(apart)
    def _():
        await_bytes(mom.at[0], mom_send.at[0])
        await_bytes(mom.at[1], mom_send.at[1])
        await_bytes(new, new_send)

    await_bytes(tile, st_own)
    await_bytes(sag.at[pl.ds(0, 63)], st_send)
    await_bytes(sag.at[pl.ds(0, 63)], st_recv)
    await_bytes(new, new_recv)


def finish(basis_in, sag, new_in, upd_out, first_out, second_out, bas, st, upd, sem):
    loads = [pltpu.make_async_copy(basis_in, bas, sem.at[0])]
    for b in range(2):
        at = pl.ds(4 * b, 4)
        loads.append(pltpu.make_async_copy(sag.at[:, at], st.at[:, at], sem.at[1 + b]))
    moves = [
        pltpu.make_async_copy(new_in.at[0], first_out, sem.at[3]),
        pltpu.make_async_copy(new_in.at[1], second_out, sem.at[4]),
    ]
    for copy in loads + moves:
        copy.start()

    row = lax.broadcasted_iota(jnp.int32, (RANK, 128), 0)
    col = lax.broadcasted_iota(jnp.int32, (RANK, 128), 1)
    loads[0].wait()
    left = []
    for s in range(2):
        hit = col == (row // 8) * 16 + row % 8 + 8 * s
        one = jnp.where(hit, -step_rate, 0.0).astype(BF16)
        left.append(jnp.dot(bas[...], one, preferred_element_type=F32).astype(BF16))
    left = jnp.concatenate(left, axis=0)

    for b in range(2):
        loads[1 + b].wait()
        right = jnp.concatenate(
            [jnp.concatenate([st[i, 4 * b + j] for i in range(8)], axis=0) for j in range(4)],
            axis=1,
        )
        both = jnp.dot(left, right, preferred_element_type=F32)
        l = [both[:RANK, 128 * j : 128 * j + 128] for j in range(4)]
        u = [both[RANK:, 128 * j : 128 * j + 128] for j in range(4)]
        tiles = [
            l[0],
            jnp.where(col < 96, u[0], l[1]),
            u[1],
            jnp.where(col < 64, l[1], l[2]),
            u[2],
            jnp.where(col < 32, l[2], l[3]),
            u[3],
        ]
        upd[b] = jnp.concatenate(tiles, axis=1).astype(BF16)
        moves.append(
            pltpu.make_async_copy(
                upd.at[b], upd_out.at[:, pl.ds(896 * b, 896)], sem.at[5 + b]
            )
        )
        moves[-1].start()
    for copy in moves:
        copy.wait()


def per_device(tokens, out_grad, basis, first_moment, second_moment):
    hbm = pl.BlockSpec(memory_space=pltpu.HBM)
    dma = pltpu.SemaphoreType.DMA
    steps, moments = pl.pallas_call(
        kernel,
        out_shape=(
            jax.ShapeDtypeStruct((64, 16, 128), BF16),
            jax.ShapeDtypeStruct((2, 8, UNIT), F32),
        ),
        in_specs=[hbm] * 5,
        out_specs=[hbm] * 2,
        scratch_shapes=[
            pltpu.VMEM((RANK, RANK), BF16),
            pltpu.VMEM((2 * TOK, D), BF16),
            pltpu.VMEM((4, 2 * TOK, SPAN), BF16),
            pltpu.VMEM((64, 16, 128), BF16),
            pltpu.VMEM((2, RANK // 2, 2 * TOK), BF16),
            pltpu.VMEM((3, NX, 16, SPAN), BF16),
            pltpu.VMEM((3, NX - 1, 16, SPAN), BF16),
            pltpu.VMEM((NZ, 16, WIN), BF16),
            pltpu.VMEM((NZ - 1, 16, WIN), BF16),
            pltpu.VMEM((NZ, 16, WIN // 2), BF16),
            pltpu.VMEM((NZ - 1, 16, WIN // 2), BF16),
            pltpu.VMEM((NZ, 32, WIN), BF16),
            pltpu.VMEM((NZ - 1, 32, WIN), BF16),
            pltpu.VMEM((NX, 8, WIN), F32),
            pltpu.VMEM((NX - 1, 8, WIN), F32),
            pltpu.VMEM((NY, 8, 256), F32),
            pltpu.VMEM((NY - 1, 8, 256), F32),
            pltpu.VMEM((16, 128), BF16),
            pltpu.VMEM((2, 8, UNIT), F32),
            pltpu.VMEM((2, 8, UNIT), F32),
            dma((3,)),
            dma((2,)), dma, dma((4,)),
            dma, dma((8,)), dma, dma((3,)),
            dma, dma,
            dma((4,)), dma((4,)),
            dma((3,)), dma((3,)),
            dma, dma,
            dma((2,)), dma((2,)),
            dma, dma,
            dma, dma, dma,
            pltpu.SemaphoreType.REGULAR,
        ],
        compiler_params=pltpu.CompilerParams(
            collective_id=0, has_side_effects=True, vmem_limit_bytes=60 << 20
        ),
    )(tokens, out_grad, basis, first_moment, second_moment)
    return pl.pallas_call(
        finish,
        out_shape=(
            jax.ShapeDtypeStruct((RANK, SPAN), BF16),
            jax.ShapeDtypeStruct((8, UNIT), F32),
            jax.ShapeDtypeStruct((8, UNIT), F32),
        ),
        in_specs=[hbm] * 3,
        out_specs=[hbm] * 3,
        scratch_shapes=[
            pltpu.VMEM((RANK, RANK), BF16),
            pltpu.VMEM((8, 8, 16, 128), BF16),
            pltpu.VMEM((2, RANK, SPAN // 2), BF16),
            dma((7,)),
        ],
        compiler_params=pltpu.CompilerParams(vmem_limit_bytes=60 << 20),
    )(basis, steps.reshape(8, 8, 16, 128), moments)


def solution(mesh):
    placed = (
        P(("dp", "fsdp"), None),
        P(("dp", "fsdp"), None),
        P("fsdp", None),
        P("dp", "fsdp"),
        P("dp", "fsdp"),
    )
    return jax.shard_map(
        per_device,
        mesh=mesh,
        in_specs=placed,
        out_specs=(P("fsdp", "dp"), P("dp", "fsdp"), P("dp", "fsdp")),
        check_vma=False,
    )
```

```python
import jax
import jax.numpy as jnp
from jax import lax
from jax.experimental import pallas as pl
from jax.experimental.pallas import tpu as pltpu
from jax.sharding import PartitionSpec as P

beta_one = 0.9
beta_two = 0.999
corr_one = 1.0 - 0.9**10
corr_two = 1.0 - 0.999**10
adam_eps = 1e-08
step_rate = 4.0

F32, BF16 = jnp.float32, jnp.bfloat16
NX, NY, NZ = 4, 8, 8
TOK = 128
D = 4096
RANK = 64
SPAN = 1792
UNIT = 224
WIN = 512
STARTS = (0, 3, 7, 10)
FAR = (4, 3, 5, 2, 6, 1, 7)


def await_bytes(ref, sem):
    pltpu.make_async_copy(ref, ref, sem).wait()


def kernel(
    tok_in, og_in, basis_in, first_in, second_in,
    sag, new_out,
    bas, tok, og, bag, cot, g, xr, zs, zr, zs3, zr3, xs3, xr3, ys, yr, tile, mom, new,
    ld_sem, core_send, core_recv, og_recv, ag_send, ag_recv, fw_send, fw_recv, cot_send, cot_recv,
    x_send, x_recv, z_send, z_recv, y_send, y_recv, mom_send, mom_recv, new_send, new_recv,
    st_send, st_recv, st_own, ready,
):
    d = lax.axis_index("dp")
    f = lax.axis_index("fsdp")
    h, c = d // 2, d % 2
    x, z, p = f // 16, (f // 2) % 8, f % 2
    y = 2 * h + p
    oc = 1 - c

    def dev(x_, y_, z_, c_):
        return ((y_ // 2) * 2 + c_, (x_ * 8 + z_) * 2 + y_ % 2)

    swap = dev(h, 2 * x + p, 4 * c + z % 4, z // 4)
    alone = jnp.logical_and(x == h, z // 4 == c)
    apart = jnp.logical_not(alone)
    other = dev(x, y, z, oc)
    xs = [dev((x + o) % 4, y, z, c) for o in range(4)]

    def plane(a, b, s):
        return dev((x + a) % 4, 2 * h + (p + s) % 2, (z + b) % 8, c)

    def remote(src, dst, send, recv, target):
        return pltpu.make_async_remote_copy(
            src_ref=src, dst_ref=dst, send_sem=send, recv_sem=recv,
            device_id=target, device_id_type=pl.DeviceIdType.MESH,
        )

    def signal(sem, target):
        pl.semaphore_signal(sem, inc=1, device_id=target, device_id_type=pl.DeviceIdType.MESH)

    barrier = pltpu.get_barrier_semaphore()
    pltpu.make_async_copy(basis_in, bas, ld_sem.at[2]).start()
    for b in FAR + (0,):
        for s in (1, 0):
            if (b, s) != (0, 0):
                signal(barrier, plane(0, b, s))
    for a in (2, 1, 3):
        for r in range(2):
            signal(barrier, dev(x, 2 * ((h + a) % 4) + r, z, c))
    for o in (2, 1, 3):
        signal(barrier, xs[o])
    signal(barrier, other)

    mine = pl.ds(pl.multiple_of(c * TOK, TOK), TOK)
    pltpu.make_async_copy(tok_in, tok.at[mine], ld_sem.at[0]).start()
    for q in range(4):
        cols = pl.ds(pl.multiple_of((2 * q + c) * SPAN, 128), SPAN)
        pltpu.make_async_copy(og_in.at[:, cols], og.at[q, mine], ld_sem.at[1]).start()

    await_bytes(bas, ld_sem.at[2])
    bt = jnp.transpose(bas[...].astype(F32))
    pieces = [bt[16 * i : 16 * i + 16] for i in range(4)]
    low = jnp.where(c == 0, pieces[0], pieces[2])
    high = jnp.where(c == 0, pieces[1], pieces[3])
    bag[f] = jnp.concatenate([low, high], axis=1).astype(BF16)

    pl.semaphore_wait(barrier, 25)

    for b in FAR + (0,):
        for s in (1, 0):
            if (b, s) != (0, 0):
                remote(bag.at[f], bag.at[f], ag_send, ag_recv.at[b], plane(0, b, s)).start()
    remote(tok_in, tok.at[mine], core_send.at[0], core_recv, other).start()
    for q in (0, 3, 1, 2):
        cols = pl.ds(pl.multiple_of((2 * q + oc) * SPAN, 128), SPAN)
        remote(og_in.at[:, cols], og.at[q, mine], core_send.at[1], og_recv.at[q], other).start()
    for b in (0, 1, 7, 2, 6, 3, 5, 4):
        await_bytes(bag.at[pl.ds(0, 2 if b else 1)], ag_recv.at[b])
        pair = bag.at[pl.ds(16 * x + 2 * ((z + 8 - b) % 8), 2)]
        for o in (2, 1, 3):
            remote(pair, pair, fw_send, fw_recv.at[o - 1], xs[o]).start()

    await_bytes(tok.at[mine], ld_sem.at[0])
    await_bytes(tok.at[mine], core_recv)
    lane = lax.broadcasted_iota(jnp.int32, (16, 128), 1)
    half = None
    for o in (0, 1, 3, 2):
        at = (x + 4 - o) % 4
        if o:
            await_bytes(bag.at[pl.ds(0, 16)], fw_recv.at[o - 1])
        tops, bottoms = [], []
        for k in range(8):
            even = bag[16 * at + 2 * k].astype(F32)
            odd = bag[16 * at + 2 * k + 1].astype(F32)
            tops.append(jnp.where(lane < 64, even, pltpu.roll(odd, 64, axis=1)).astype(BF16))
            bottoms.append(jnp.where(lane < 64, pltpu.roll(even, 64, axis=1), odd).astype(BF16))
        basis_t = jnp.concatenate(
            [jnp.concatenate(tops, axis=1), jnp.concatenate(bottoms, axis=1)], axis=0
        )
        term = lax.dot_general(
            basis_t,
            tok[:, pl.ds(pl.multiple_of(1024 * at, 1024), 1024)],
            (((1,), (1,)), ((), ())),
            preferred_element_type=F32,
        )
        half = term if half is None else half + term
    cot[c] = half.astype(BF16)
    remote(cot.at[c], cot.at[c], cot_send, cot_recv, other).start()
    await_bytes(cot.at[c], cot_recv)
    coords_t = cot[...].reshape(RANK, 2 * TOK)

    for o in FAR:
        signal(ready, dev(x, (y + o) % 8, z, c))

    await_bytes(og.at[:, mine], ld_sem.at[1])
    for q in (0, 3, 1, 2):
        await_bytes(og.at[q, mine], og_recv.at[q])
        part = jnp.dot(coords_t, og[q], preferred_element_type=F32)
        if q == 3:
            for to in range(8):
                s, start = to // 4, 128 * STARTS[to % 4]
                zs3[to] = jnp.concatenate(
                    [part[16 * i + 8 * s : 16 * i + 8 * s + 8, start : start + WIN] for i in range(4)],
                    axis=0,
                ).astype(BF16)
            for o in FAR:
                to = (z + o) % 8
                remote(
                    zs3.at[to], zr3.at[o - 1], z_send.at[3], z_recv.at[3], dev(x, y, to, c)
                ).start()
        else:
            part = part.astype(BF16)
            for i in range(4):
                g[q, i] = part[16 * i : 16 * i + 16]
            for o in (2, 1, 3):
                remote(
                    g.at[q, (x + o) % 4], xr.at[q, o - 1], x_send.at[q], x_recv.at[q], xs[o]
                ).start()

    def along_z(q):
        await_bytes(xr.at[q], x_recv.at[q])
        total = g[q, x].astype(F32)
        for o in range(3):
            total = total + xr[q, o].astype(F32)
        for to in range(8):
            s, start = to // 4, 128 * STARTS[to % 4]
            rows = total[8 * s : 8 * s + 8]
            zs[q, to] = jnp.concatenate(
                [rows[:, start : start + 256], rows[:, start + 256 : start + 512]], axis=0
            ).astype(BF16)
        for o in FAR:
            to = (z + o) % 8
            remote(
                zs.at[q, to], zr.at[q, o - 1], z_send.at[q], z_recv.at[q], dev(x, y, to, c)
            ).start()

    along_z(0)

    pl.semaphore_wait(ready, 7)

    @pl.when(apart)
    def _():
        remote(first_in, mom.at[0], mom_send.at[0], mom_recv.at[0], swap).start()
        remote(second_in, mom.at[1], mom_send.at[1], mom_recv.at[1], swap).start()

    @pl.when(alone)
    def _():
        pltpu.make_async_copy(first_in, mom.at[0], mom_recv.at[0]).start()
        pltpu.make_async_copy(second_in, mom.at[1], mom_recv.at[1]).start()

    along_z(1)

    await_bytes(zr3, z_recv.at[3])
    total = zs3[z].astype(F32)
    for o in range(7):
        total = total + zr3[o].astype(F32)
    for i in range(4):
        xs3[i] = total[8 * i : 8 * i + 8]
    for o in (2, 1, 3):
        remote(xs3.at[(x + o) % 4], xr3.at[o - 1], x_send.at[3], x_recv.at[3], xs[o]).start()

    along_z(2)

    def along_y(total, q):
        total = pltpu.roll(total, 512 - 64 * (z % 2), axis=1)
        blocks = [total[:, :256], pltpu.roll(total, 512 - UNIT, axis=1)[:, :256]]
        for r in range(2):
            to = 2 * q + r
            ys[to] = blocks[r]

            @pl.when(y != to)
            def _():
                slot = (to + 8 - y) % 8 - 1
                remote(ys.at[to], yr.at[slot], y_send, y_recv, dev(x, to, z, c)).start()

    def end_z(q):
        await_bytes(zr.at[q], z_recv.at[q])
        total = zs[q, z].astype(F32)
        for o in range(7):
            total = total + zr[q, o].astype(F32)
        along_y(jnp.concatenate([total[:8], total[8:]], axis=1), q)

    end_z(0)
    end_z(1)
    await_bytes(xr3, x_recv.at[3])
    total = xs3[x]
    for o in range(3):
        total = total + xr3[o]
    along_y(total, 3)

    end_z(2)

    await_bytes(mom.at[0], mom_recv.at[0])
    await_bytes(mom.at[1], mom_recv.at[1])
    await_bytes(yr, y_recv)
    total = ys[y]
    for o in range(7):
        total = total + yr[o]
    grad = total[:, :UNIT]
    new_first = beta_one * mom[0] + (1.0 - beta_one) * grad
    new_second = beta_two * mom[1] + (1.0 - beta_two) * grad * grad
    new[0] = new_first
    new[1] = new_second

    @pl.when(apart)
    def _():
        remote(new, new_out, new_send, new_recv, swap).start()

    @pl.when(alone)
    def _():
        pltpu.make_async_copy(new, new_out, new_recv).start()

    step = new_first / corr_one / (jnp.sqrt(new_second / corr_two) + adam_eps)
    step = jnp.concatenate([step, jnp.zeros((8, 256 - UNIT), F32)], axis=1)
    step = pltpu.roll(step, (96 * (2 * z + p)) % 128, axis=1)
    tile[...] = jnp.concatenate([step[:, :128], step[:, 128:]], axis=0).astype(BF16)
    offsets = [(a, b, s) for a in range(4) for b in range(8) for s in range(2)][1:]
    offsets.sort(key=lambda o: -(min(o[0], 4 - o[0]) + min(o[1], 8 - o[1]) + o[2]))
    for o in offsets:
        remote(tile, sag.at[f], st_send, st_recv, plane(*o)).start()
    pltpu.make_async_copy(tile, sag.at[f], st_own).start()

    await_bytes(bag.at[pl.ds(0, 15)], ag_send)
    await_bytes(bag.at[pl.ds(0, 48)], fw_send)
    await_bytes(tok.at[mine], core_send.at[0])
    await_bytes(og.at[:, mine], core_send.at[1])
    await_bytes(cot.at[c], cot_send)
    for q in range(3):
        await_bytes(xr.at[q], x_send.at[q])
        await_bytes(zr.at[q], z_send.at[q])
    await_bytes(zr3, z_send.at[3])
    await_bytes(xr3, x_send.at[3])
    await_bytes(yr, y_send)

    @pl.when(apart)
    def _():
        await_bytes(mom.at[0], mom_send.at[0])
        await_bytes(mom.at[1], mom_send.at[1])
        await_bytes(new, new_send)

    await_bytes(tile, st_own)
    await_bytes(sag.at[pl.ds(0, 63)], st_send)
    await_bytes(sag.at[pl.ds(0, 63)], st_recv)
    await_bytes(new, new_recv)


def finish(basis_in, sag, new_in, upd_out, first_out, second_out, bas, st, upd, sem):
    loads = [pltpu.make_async_copy(basis_in, bas, sem.at[0])]
    for b in range(2):
        at = pl.ds(4 * b, 4)
        loads.append(pltpu.make_async_copy(sag.at[:, at], st.at[:, at], sem.at[1 + b]))
    moves = [
        pltpu.make_async_copy(new_in.at[0], first_out, sem.at[3]),
        pltpu.make_async_copy(new_in.at[1], second_out, sem.at[4]),
    ]
    for copy in loads + moves:
        copy.start()

    row = lax.broadcasted_iota(jnp.int32, (RANK, 128), 0)
    col = lax.broadcasted_iota(jnp.int32, (RANK, 128), 1)
    loads[0].wait()
    left = []
    for s in range(2):
        hit = col == (row // 8) * 16 + row % 8 + 8 * s
        one = jnp.where(hit, -step_rate, 0.0).astype(BF16)
        left.append(jnp.dot(bas[...], one, preferred_element_type=F32).astype(BF16))
    left = jnp.concatenate(left, axis=0)

    for b in range(2):
        loads[1 + b].wait()
        right = jnp.concatenate(
            [jnp.concatenate([st[i, 4 * b + j] for i in range(8)], axis=0) for j in range(4)],
            axis=1,
        )
        both = jnp.dot(left, right, preferred_element_type=F32)
        l = [both[:RANK, 128 * j : 128 * j + 128] for j in range(4)]
        u = [both[RANK:, 128 * j : 128 * j + 128] for j in range(4)]
        tiles = [
            l[0],
            jnp.where(col < 96, u[0], l[1]),
            u[1],
            jnp.where(col < 64, l[1], l[2]),
            u[2],
            jnp.where(col < 32, l[2], l[3]),
            u[3],
        ]
        upd[b] = jnp.concatenate(tiles, axis=1).astype(BF16)
        moves.append(
            pltpu.make_async_copy(
                upd.at[b], upd_out.at[:, pl.ds(896 * b, 896)], sem.at[5 + b]
            )
        )
        moves[-1].start()
    for copy in moves:
        copy.wait()


def per_device(tokens, out_grad, basis, first_moment, second_moment):
    hbm = pl.BlockSpec(memory_space=pltpu.HBM)
    dma = pltpu.SemaphoreType.DMA
    steps, moments = pl.pallas_call(
        kernel,
        out_shape=(
            jax.ShapeDtypeStruct((64, 16, 128), BF16),
            jax.ShapeDtypeStruct((2, 8, UNIT), F32),
        ),
        in_specs=[hbm] * 5,
        out_specs=[hbm] * 2,
        scratch_shapes=[
            pltpu.VMEM((RANK, RANK), BF16),
            pltpu.VMEM((2 * TOK, D), BF16),
            pltpu.VMEM((4, 2 * TOK, SPAN), BF16),
            pltpu.VMEM((64, 16, 128), BF16),
            pltpu.VMEM((2, RANK // 2, 2 * TOK), BF16),
            pltpu.VMEM((3, NX, 16, SPAN), BF16),
            pltpu.VMEM((3, NX - 1, 16, SPAN), BF16),
            pltpu.VMEM((3, NZ, 16, WIN // 2), BF16),
            pltpu.VMEM((3, NZ - 1, 16, WIN // 2), BF16),
            pltpu.VMEM((NZ, 32, WIN), BF16),
            pltpu.VMEM((NZ - 1, 32, WIN), BF16),
            pltpu.VMEM((NX, 8, WIN), F32),
            pltpu.VMEM((NX - 1, 8, WIN), F32),
            pltpu.VMEM((NY, 8, 256), F32),
            pltpu.VMEM((NY - 1, 8, 256), F32),
            pltpu.VMEM((16, 128), BF16),
            pltpu.VMEM((2, 8, UNIT), F32),
            pltpu.VMEM((2, 8, UNIT), F32),
            dma((3,)),
            dma((2,)), dma, dma((4,)),
            dma, dma((8,)), dma, dma((3,)),
            dma, dma,
            dma((4,)), dma((4,)),
            dma((4,)), dma((4,)),
            dma, dma,
            dma((2,)), dma((2,)),
            dma, dma,
            dma, dma, dma,
            pltpu.SemaphoreType.REGULAR,
        ],
        compiler_params=pltpu.CompilerParams(
            collective_id=0, has_side_effects=True, vmem_limit_bytes=60 << 20
        ),
    )(tokens, out_grad, basis, first_moment, second_moment)
    return pl.pallas_call(
        finish,
        out_shape=(
            jax.ShapeDtypeStruct((RANK, SPAN), BF16),
            jax.ShapeDtypeStruct((8, UNIT), F32),
            jax.ShapeDtypeStruct((8, UNIT), F32),
        ),
        in_specs=[hbm] * 3,
        out_specs=[hbm] * 3,
        scratch_shapes=[
            pltpu.VMEM((RANK, RANK), BF16),
            pltpu.VMEM((8, 8, 16, 128), BF16),
            pltpu.VMEM((2, RANK, SPAN // 2), BF16),
            dma((7,)),
        ],
        compiler_params=pltpu.CompilerParams(vmem_limit_bytes=60 << 20),
    )(basis, steps.reshape(8, 8, 16, 128), moments)


def solution(mesh):
    placed = (
        P(("dp", "fsdp"), None),
        P(("dp", "fsdp"), None),
        P("fsdp", None),
        P("dp", "fsdp"),
        P("dp", "fsdp"),
    )
    return jax.shard_map(
        per_device,
        mesh=mesh,
        in_specs=placed,
        out_specs=(P("fsdp", "dp"), P("dp", "fsdp"), P("dp", "fsdp")),
        check_vma=False,
    )
```

```python
import jax
import jax.numpy as jnp
from jax import lax
from jax.experimental import pallas as pl
from jax.experimental.pallas import tpu as pltpu
from jax.sharding import PartitionSpec as P

beta_one = 0.9
beta_two = 0.999
corr_one = 1.0 - 0.9**10
corr_two = 1.0 - 0.999**10
adam_eps = 1e-08
step_rate = 4.0

F32, BF16 = jnp.float32, jnp.bfloat16
NX, NY, NZ = 4, 8, 8
TOK = 128
D = 4096
RANK = 64
SPAN = 1792
UNIT = 224
WIN = 512
STARTS = (0, 3, 7, 10)
FAR = (4, 3, 5, 2, 6, 1, 7)


def await_bytes(ref, sem):
    pltpu.make_async_copy(ref, ref, sem).wait()


def kernel(
    tok_in, og_in, basis_in, first_in, second_in,
    sag, new_out,
    bas, tok, og, bag, cot, g, xr, zs, zr, zs3, zr3, xs3, xr3, ys, yr, tile, mom, new,
    ld_sem, core_send, core_recv, og_recv, ag_send, ag_recv, fw_send, fw_recv, cot_send, cot_recv,
    x_send, x_recv, z_send, z_recv, y_send, y_recv, mom_send, mom_recv, new_send, new_recv,
    st_send, st_recv, st_own, ready,
):
    d = lax.axis_index("dp")
    f = lax.axis_index("fsdp")
    h, c = d // 2, d % 2
    x, z, p = f // 16, (f // 2) % 8, f % 2
    y = 2 * h + p
    oc = 1 - c

    def dev(x_, y_, z_, c_):
        return ((y_ // 2) * 2 + c_, (x_ * 8 + z_) * 2 + y_ % 2)

    rx, kz = (x + 2) % 4, (z + 2) % 4
    owner = dev(h, 2 * rx + p, 4 * c + kz, z // 4)
    taker = dev((h + 2) % 4, 2 * x + p, 4 * c + kz, z // 4)
    role = 16 * rx + 8 * (z // 4) + 2 * kz + p
    other = dev(x, y, z, oc)
    xs = [dev((x + o) % 4, y, z, c) for o in range(4)]

    def plane(a, b, s):
        return dev((x + a) % 4, 2 * h + (p + s) % 2, (z + b) % 8, c)

    def remote(src, dst, send, recv, target):
        return pltpu.make_async_remote_copy(
            src_ref=src, dst_ref=dst, send_sem=send, recv_sem=recv,
            device_id=target, device_id_type=pl.DeviceIdType.MESH,
        )

    def signal(sem, target):
        pl.semaphore_signal(sem, inc=1, device_id=target, device_id_type=pl.DeviceIdType.MESH)

    barrier = pltpu.get_barrier_semaphore()
    pltpu.make_async_copy(basis_in, bas, ld_sem.at[2]).start()
    for b in FAR + (0,):
        for s in (1, 0):
            if (b, s) != (0, 0):
                signal(barrier, plane(0, b, s))
    for a in (2, 1, 3):
        for r in range(2):
            signal(barrier, dev(x, 2 * ((h + a) % 4) + r, z, c))
    for o in (2, 1, 3):
        signal(barrier, xs[o])
    signal(barrier, other)

    mine = pl.ds(pl.multiple_of(c * TOK, TOK), TOK)
    pltpu.make_async_copy(tok_in, tok.at[mine], ld_sem.at[0]).start()
    for q in range(4):
        cols = pl.ds(pl.multiple_of((2 * q + c) * SPAN, 128), SPAN)
        pltpu.make_async_copy(og_in.at[:, cols], og.at[q, mine], ld_sem.at[1]).start()

    await_bytes(bas, ld_sem.at[2])
    bt = jnp.transpose(bas[...].astype(F32))
    pieces = [bt[16 * i : 16 * i + 16] for i in range(4)]
    low = jnp.where(c == 0, pieces[0], pieces[2])
    high = jnp.where(c == 0, pieces[1], pieces[3])
    bag[f] = jnp.concatenate([low, high], axis=1).astype(BF16)

    pl.semaphore_wait(barrier, 25)

    for b in FAR + (0,):
        for s in (1, 0):
            if (b, s) != (0, 0):
                remote(bag.at[f], bag.at[f], ag_send, ag_recv.at[b], plane(0, b, s)).start()
    remote(tok_in, tok.at[mine], core_send.at[0], core_recv, other).start()
    for q in (0, 3, 1, 2):
        cols = pl.ds(pl.multiple_of((2 * q + oc) * SPAN, 128), SPAN)
        remote(og_in.at[:, cols], og.at[q, mine], core_send.at[1], og_recv.at[q], other).start()
    for b in (0, 1, 7, 2, 6, 3, 5, 4):
        await_bytes(bag.at[pl.ds(0, 2 if b else 1)], ag_recv.at[b])
        pair = bag.at[pl.ds(16 * x + 2 * ((z + 8 - b) % 8), 2)]
        for o in (2, 1, 3):
            remote(pair, pair, fw_send, fw_recv.at[o - 1], xs[o]).start()

    await_bytes(tok.at[mine], ld_sem.at[0])
    await_bytes(tok.at[mine], core_recv)
    lane = lax.broadcasted_iota(jnp.int32, (16, 128), 1)
    half = None
    for o in (0, 1, 3, 2):
        at = (x + 4 - o) % 4
        if o:
            await_bytes(bag.at[pl.ds(0, 16)], fw_recv.at[o - 1])
        tops, bottoms = [], []
        for k in range(8):
            even = bag[16 * at + 2 * k].astype(F32)
            odd = bag[16 * at + 2 * k + 1].astype(F32)
            tops.append(jnp.where(lane < 64, even, pltpu.roll(odd, 64, axis=1)).astype(BF16))
            bottoms.append(jnp.where(lane < 64, pltpu.roll(even, 64, axis=1), odd).astype(BF16))
        basis_t = jnp.concatenate(
            [jnp.concatenate(tops, axis=1), jnp.concatenate(bottoms, axis=1)], axis=0
        )
        term = lax.dot_general(
            basis_t,
            tok[:, pl.ds(pl.multiple_of(1024 * at, 1024), 1024)],
            (((1,), (1,)), ((), ())),
            preferred_element_type=F32,
        )
        half = term if half is None else half + term
    cot[c] = half.astype(BF16)
    remote(cot.at[c], cot.at[c], cot_send, cot_recv, other).start()
    await_bytes(cot.at[c], cot_recv)
    coords_t = cot[...].reshape(RANK, 2 * TOK)

    for o in FAR:
        signal(ready, dev(x, (y + o) % 8, z, c))

    await_bytes(og.at[:, mine], ld_sem.at[1])
    for q in (0, 3, 1, 2):
        await_bytes(og.at[q, mine], og_recv.at[q])
        part = jnp.dot(coords_t, og[q], preferred_element_type=F32)
        if q == 3:
            for to in range(8):
                s, start = to // 4, 128 * STARTS[(to + 2) % 4]
                zs3[to] = jnp.concatenate(
                    [part[16 * i + 8 * s : 16 * i + 8 * s + 8, start : start + WIN] for i in range(4)],
                    axis=0,
                ).astype(BF16)
            for o in FAR:
                to = (z + o) % 8
                remote(
                    zs3.at[to], zr3.at[o - 1], z_send.at[3], z_recv.at[3], dev(x, y, to, c)
                ).start()
        else:
            part = part.astype(BF16)
            for i in range(4):
                g[q, i] = part[16 * i : 16 * i + 16]
            for o in (2, 1, 3):
                remote(
                    g.at[q, (rx + o) % 4], xr.at[q, o - 1], x_send.at[q], x_recv.at[q], xs[o]
                ).start()

    def along_z(q):
        await_bytes(xr.at[q], x_recv.at[q])
        total = g[q, rx].astype(F32)
        for o in range(3):
            total = total + xr[q, o].astype(F32)
        for to in range(8):
            s, start = to // 4, 128 * STARTS[(to + 2) % 4]
            rows = total[8 * s : 8 * s + 8]
            zs[q, to] = jnp.concatenate(
                [rows[:, start : start + 256], rows[:, start + 256 : start + 512]], axis=0
            ).astype(BF16)
        for o in FAR:
            to = (z + o) % 8
            remote(
                zs.at[q, to], zr.at[q, o - 1], z_send.at[q], z_recv.at[q], dev(x, y, to, c)
            ).start()

    along_z(0)

    pl.semaphore_wait(ready, 7)

    remote(first_in, mom.at[0], mom_send.at[0], mom_recv.at[0], taker).start()
    remote(second_in, mom.at[1], mom_send.at[1], mom_recv.at[1], taker).start()

    along_z(1)

    await_bytes(zr3, z_recv.at[3])
    total = zs3[z].astype(F32)
    for o in range(7):
        total = total + zr3[o].astype(F32)
    for i in range(4):
        xs3[i] = total[8 * i : 8 * i + 8]
    for o in (2, 1, 3):
        remote(xs3.at[(rx + o) % 4], xr3.at[o - 1], x_send.at[3], x_recv.at[3], xs[o]).start()

    along_z(2)

    def along_y(total, q):
        total = pltpu.roll(total, 512 - 64 * (z % 2), axis=1)
        blocks = [total[:, :256], pltpu.roll(total, 512 - UNIT, axis=1)[:, :256]]
        for r in range(2):
            to = 2 * q + r
            ys[to] = blocks[r]

            @pl.when(y != to)
            def _():
                slot = (to + 8 - y) % 8 - 1
                remote(ys.at[to], yr.at[slot], y_send, y_recv, dev(x, to, z, c)).start()

    def end_z(q):
        await_bytes(zr.at[q], z_recv.at[q])
        total = zs[q, z].astype(F32)
        for o in range(7):
            total = total + zr[q, o].astype(F32)
        along_y(jnp.concatenate([total[:8], total[8:]], axis=1), q)

    end_z(0)
    end_z(1)
    await_bytes(xr3, x_recv.at[3])
    total = xs3[rx]
    for o in range(3):
        total = total + xr3[o]
    along_y(total, 3)

    end_z(2)

    await_bytes(mom.at[0], mom_recv.at[0])
    await_bytes(mom.at[1], mom_recv.at[1])
    await_bytes(yr, y_recv)
    total = ys[y]
    for o in range(7):
        total = total + yr[o]
    grad = total[:, :UNIT]
    new_first = beta_one * mom[0] + (1.0 - beta_one) * grad
    new_second = beta_two * mom[1] + (1.0 - beta_two) * grad * grad
    new[0] = new_first
    new[1] = new_second

    remote(new, new_out, new_send, new_recv, owner).start()

    step = new_first / corr_one / (jnp.sqrt(new_second / corr_two) + adam_eps)
    step = jnp.concatenate([step, jnp.zeros((8, 256 - UNIT), F32)], axis=1)
    step = pltpu.roll(step, (96 * (2 * z + p)) % 128, axis=1)
    tile[...] = jnp.concatenate([step[:, :128], step[:, 128:]], axis=0).astype(BF16)
    offsets = [(a, b, s) for a in range(4) for b in range(8) for s in range(2)][1:]
    offsets.sort(key=lambda o: -(min(o[0], 4 - o[0]) + min(o[1], 8 - o[1]) + o[2]))
    for o in offsets:
        remote(tile, sag.at[role], st_send, st_recv, plane(*o)).start()
    pltpu.make_async_copy(tile, sag.at[role], st_own).start()

    await_bytes(bag.at[pl.ds(0, 15)], ag_send)
    await_bytes(bag.at[pl.ds(0, 48)], fw_send)
    await_bytes(tok.at[mine], core_send.at[0])
    await_bytes(og.at[:, mine], core_send.at[1])
    await_bytes(cot.at[c], cot_send)
    for q in range(3):
        await_bytes(xr.at[q], x_send.at[q])
        await_bytes(zr.at[q], z_send.at[q])
    await_bytes(zr3, z_send.at[3])
    await_bytes(xr3, x_send.at[3])
    await_bytes(yr, y_send)

    await_bytes(mom.at[0], mom_send.at[0])
    await_bytes(mom.at[1], mom_send.at[1])
    await_bytes(new, new_send)
    await_bytes(tile, st_own)
    await_bytes(sag.at[pl.ds(0, 63)], st_send)
    await_bytes(sag.at[pl.ds(0, 63)], st_recv)
    await_bytes(new, new_recv)


def finish(basis_in, sag, new_in, upd_out, first_out, second_out, bas, st, upd, sem):
    loads = [pltpu.make_async_copy(basis_in, bas, sem.at[0])]
    for b in range(2):
        at = pl.ds(4 * b, 4)
        loads.append(pltpu.make_async_copy(sag.at[:, at], st.at[:, at], sem.at[1 + b]))
    moves = [
        pltpu.make_async_copy(new_in.at[0], first_out, sem.at[3]),
        pltpu.make_async_copy(new_in.at[1], second_out, sem.at[4]),
    ]
    for copy in loads + moves:
        copy.start()

    row = lax.broadcasted_iota(jnp.int32, (RANK, 128), 0)
    col = lax.broadcasted_iota(jnp.int32, (RANK, 128), 1)
    loads[0].wait()
    left = []
    for s in range(2):
        hit = col == (row // 8) * 16 + row % 8 + 8 * s
        one = jnp.where(hit, -step_rate, 0.0).astype(BF16)
        left.append(jnp.dot(bas[...], one, preferred_element_type=F32).astype(BF16))
    left = jnp.concatenate(left, axis=0)

    for b in range(2):
        loads[1 + b].wait()
        right = jnp.concatenate(
            [jnp.concatenate([st[i, 4 * b + j] for i in range(8)], axis=0) for j in range(4)],
            axis=1,
        )
        both = jnp.dot(left, right, preferred_element_type=F32)
        l = [both[:RANK, 128 * j : 128 * j + 128] for j in range(4)]
        u = [both[RANK:, 128 * j : 128 * j + 128] for j in range(4)]
        tiles = [
            l[0],
            jnp.where(col < 96, u[0], l[1]),
            u[1],
            jnp.where(col < 64, l[1], l[2]),
            u[2],
            jnp.where(col < 32, l[2], l[3]),
            u[3],
        ]
        upd[b] = jnp.concatenate(tiles, axis=1).astype(BF16)
        moves.append(
            pltpu.make_async_copy(
                upd.at[b], upd_out.at[:, pl.ds(896 * b, 896)], sem.at[5 + b]
            )
        )
        moves[-1].start()
    for copy in moves:
        copy.wait()


def per_device(tokens, out_grad, basis, first_moment, second_moment):
    hbm = pl.BlockSpec(memory_space=pltpu.HBM)
    dma = pltpu.SemaphoreType.DMA
    steps, moments = pl.pallas_call(
        kernel,
        out_shape=(
            jax.ShapeDtypeStruct((64, 16, 128), BF16),
            jax.ShapeDtypeStruct((2, 8, UNIT), F32),
        ),
        in_specs=[hbm] * 5,
        out_specs=[hbm] * 2,
        scratch_shapes=[
            pltpu.VMEM((RANK, RANK), BF16),
            pltpu.VMEM((2 * TOK, D), BF16),
            pltpu.VMEM((4, 2 * TOK, SPAN), BF16),
            pltpu.VMEM((64, 16, 128), BF16),
            pltpu.VMEM((2, RANK // 2, 2 * TOK), BF16),
            pltpu.VMEM((3, NX, 16, SPAN), BF16),
            pltpu.VMEM((3, NX - 1, 16, SPAN), BF16),
            pltpu.VMEM((3, NZ, 16, WIN // 2), BF16),
            pltpu.VMEM((3, NZ - 1, 16, WIN // 2), BF16),
            pltpu.VMEM((NZ, 32, WIN), BF16),
            pltpu.VMEM((NZ - 1, 32, WIN), BF16),
            pltpu.VMEM((NX, 8, WIN), F32),
            pltpu.VMEM((NX - 1, 8, WIN), F32),
            pltpu.VMEM((NY, 8, 256), F32),
            pltpu.VMEM((NY - 1, 8, 256), F32),
            pltpu.VMEM((16, 128), BF16),
            pltpu.VMEM((2, 8, UNIT), F32),
            pltpu.VMEM((2, 8, UNIT), F32),
            dma((3,)),
            dma((2,)), dma, dma((4,)),
            dma, dma((8,)), dma, dma((3,)),
            dma, dma,
            dma((4,)), dma((4,)),
            dma((4,)), dma((4,)),
            dma, dma,
            dma((2,)), dma((2,)),
            dma, dma,
            dma, dma, dma,
            pltpu.SemaphoreType.REGULAR,
        ],
        compiler_params=pltpu.CompilerParams(
            collective_id=0, has_side_effects=True, vmem_limit_bytes=60 << 20
        ),
    )(tokens, out_grad, basis, first_moment, second_moment)
    return pl.pallas_call(
        finish,
        out_shape=(
            jax.ShapeDtypeStruct((RANK, SPAN), BF16),
            jax.ShapeDtypeStruct((8, UNIT), F32),
            jax.ShapeDtypeStruct((8, UNIT), F32),
        ),
        in_specs=[hbm] * 3,
        out_specs=[hbm] * 3,
        scratch_shapes=[
            pltpu.VMEM((RANK, RANK), BF16),
            pltpu.VMEM((8, 8, 16, 128), BF16),
            pltpu.VMEM((2, RANK, SPAN // 2), BF16),
            dma((7,)),
        ],
        compiler_params=pltpu.CompilerParams(vmem_limit_bytes=60 << 20),
    )(basis, steps.reshape(8, 8, 16, 128), moments)


def solution(mesh):
    placed = (
        P(("dp", "fsdp"), None),
        P(("dp", "fsdp"), None),
        P("fsdp", None),
        P("dp", "fsdp"),
        P("dp", "fsdp"),
    )
    return jax.shard_map(
        per_device,
        mesh=mesh,
        in_specs=placed,
        out_specs=(P("fsdp", "dp"), P("dp", "fsdp"), P("dp", "fsdp")),
        check_vma=False,
    )
```
